32 devices in a mesh: groups: 2 (over x), dp: 16 (over z, y, core).
Axes of the slice: x: 2, y: 2, z: 4, core: 2. Of those that a mesh axis runs over, the one named last changes fastest.
Arguments:
- tokens: bfloat16 [256, 16384], P(('groups', 'dp')), parts along dimension 0, may hold values from -6 to 6
- gain: bfloat16 [16384], replicated, may hold values from 0.099609375 to 1.8984375
- gate_weight: bfloat16 [16384, 8192], P(None, 'dp'), may hold values from -0.046875 to 0.046875
- up_weight: bfloat16 [16384, 8192], P(None, 'dp'), may hold values from -0.046875 to 0.046875
- down_weight: bfloat16 [8192, 16384], P(None, 'dp'), may hold values from -0.125 to 0.125
Outputs:
- mixed: bfloat16 [256, 16384], P(('groups', 'dp')), parts along dimension 0
The draws below stay inside these ranges and needn't reach their ends.
There are 2 independent parts, one for each index of `groups`. The reference program is written for one: setup_inputs(seed, part) draws one part's arguments, and reference() takes and returns one part's arrays. A program takes and returns all parts, laid end to end along the dimension named above; an argument that names none is the same for every part. Nothing has to cross between parts.
All inputs are finite; a program needn't handle non-finite values.
Results may differ from the reference program's by a relative error of at most 0.006.
Values may be sent and summed in bfloat16 or wider, within the bound.
A program may use at most 128 MiB of HBM per device.

```python
import jax
import jax.numpy as jnp
from jax import lax

D = 16384
FF = 8192
TOKENS = 128


def block_scale(key, shape, split, smallest, largest):
    factor_of, own = 1.0, jax.random.fold_in(key, 6)
    for dim, shards_of in split:
        heights = jnp.exp(jax.random.uniform(jax.random.fold_in(own, dim), (shards_of,), jnp.float32, smallest / len(split), largest / len(split)))
        factor_of = factor_of * jnp.repeat(heights, shape[dim] // shards_of).reshape([-1 if axis == dim else 1 for axis in range(len(shape))])
    return factor_of


def gaussian(stream_key, shape, deviation, limit, pieces=(), held_as=jnp.bfloat16):
    drawn = jax.random.normal(stream_key, shape, jnp.float32) * deviation
    if len(pieces) > 0:
        drawn = block_scale(stream_key, shape, pieces, -0.22, 0.18) * drawn
    return jnp.clip(drawn, min=-limit, max=limit).astype(held_as)


def setup_inputs(seed: int = 0, part: int = 0) -> dict:
    key_list = jax.random.split(jax.random.key(seed), 6)
    part_splits = jax.random.split(jax.random.fold_in(key_list[5], part), 6)
    tokens = gaussian(part_splits[0], (TOKENS, D), 1.0, 6.0, ((0, 16),))
    gain = jnp.clip(1.0 + 0.18 * jax.random.normal(key_list[1], (D,), jnp.float32), 0.099609375, 1.8984375).astype(jnp.bfloat16)
    gate_weight = gaussian(key_list[2], (D, FF), D ** -0.5, 0.046875, ((1, 16),))
    up_weight = gaussian(key_list[3], (D, FF), D ** -0.5, 0.046875, ((1, 16),))
    down_weight = gaussian(key_list[4], (FF, D), (FF // 4) ** -0.5, 0.125, ((1, 16),))
    return {"tokens": tokens, "gain": gain, "gate_weight": gate_weight, "up_weight": up_weight, "down_weight": down_weight}


def reference(tokens, gain, gate_weight, up_weight, down_weight):
    wide = tokens.astype(jnp.float32)
    scale = jax.lax.rsqrt(lax.optimization_barrier(jnp.mean(wide * wide, axis=-1, keepdims=True)) + 1e-05)
    normed = (wide * scale * gain.astype(jnp.float32)).astype(jnp.bfloat16)
    gate = jnp.dot(normed, gate_weight, preferred_element_type=jnp.float32)
    up = jnp.dot(normed, up_weight, preferred_element_type=jnp.float32)
    hidden = (jax.nn.silu(gate) * up).astype(jnp.bfloat16)
    total = jnp.dot(hidden, down_weight, preferred_element_type=jnp.float32)
    return (wide + total).astype(jnp.bfloat16)
```

```python
import functools

import jax
import jax.numpy as jnp
from jax import lax
from jax.experimental import pallas as pl
from jax.experimental.pallas import tpu as pltpu
from jax.sharding import PartitionSpec as P

MESH = pl.DeviceIdType.MESH
CHUNKS = 8
EARLY = 4
DOWN_LOADS = 4
F32 = jnp.float32
BF16 = jnp.bfloat16


def chip_at(place, chips):
    if chips > 8:
        return place
    half = chips // 2
    back = place // half
    return (1 - back) * 2 * place + back * (2 * (chips - 1 - place) + 1)


def place_of(chip, chips):
    if chips > 8:
        return chip
    odd, rank = chip % 2, chip // 2
    return rank + odd * (chips - 1 - 2 * rank)


def block_kernel(
    n,
    tokens, gain, gate, up, down, out,
    raw, scales, gate_v, up_v, down_v, gate_acc, up_acc, hid, acc, stage,
    own_sem, gate_sem, up_sem, down_sem, scale_send, scale_recv,
    ring_recv, ring_send, sib_recv, sib_send,
    hid_recv, hid_send, hidsib_recv, hidsib_send,
    out_send, out_recv, out_own,
):
    chips = n // 2
    hops = chips // 2
    rows, width = tokens.shape
    ffl = gate.shape[1]
    cols = down.shape[1]
    depth = width // CHUNKS
    part = depth // hops
    total_rows = n * rows
    parts = hid.shape[2]
    ffe = ffl // parts
    down_rows = down.shape[0] // DOWN_LOADS

    me = lax.axis_index("dp")
    core = me % 2
    p = place_of(me // 2, chips)
    sib = me + 1 - 2 * core
    right = 2 * chip_at((p + 1) % chips, chips) + core
    left = 2 * chip_at((p + chips - 1) % chips, chips) + core
    reach = (hops - core, hops - 1 + core)

    own = pltpu.make_async_copy(tokens, raw.at[core, p], own_sem)
    own.start()

    def weight_copies(q):
        here = pl.ds(q * depth, depth)
        return (
            pltpu.make_async_copy(gate.at[here], gate_v.at[here], gate_sem.at[q]),
            pltpu.make_async_copy(up.at[here], up_v.at[here], up_sem.at[q]),
        )

    def down_copy(i):
        here = pl.ds(i * down_rows, down_rows)
        return pltpu.make_async_copy(down.at[here], down_v.at[here], down_sem.at[i])

    barrier = pltpu.get_barrier_semaphore()

    @pl.loop(1, n)
    def _(i):
        pl.semaphore_signal(barrier, inc=1, device_id={"dp": (me + i) % n}, device_id_type=MESH)

    for q in range(EARLY):
        for copy in weight_copies(q):
            copy.start()

    own.wait()
    squares = jnp.zeros((rows, 128), F32)
    step = 2048

    def add_squares(i, squares):
        wide = raw[core, p, :, pl.ds(i * step, step)].astype(F32)
        wide = wide * wide
        for b in range(step // 128):
            squares = squares + wide[:, b * 128 : (b + 1) * 128]
        return squares

    squares = lax.fori_loop(0, width // step, add_squares, squares)
    mean = jnp.sum(squares, axis=1, keepdims=True) / width
    scales[me] = jnp.broadcast_to(lax.rsqrt(mean + 1e-05), (rows, 128))
    pl.semaphore_wait(barrier, n - 1)

    def ring(k, origin, q):
        return raw.at[k, origin, :, pl.ds(q * depth, depth)]

    def send_ring(r, q, s, origin):
        pltpu.make_async_remote_copy(
            ring(core, origin, q), ring(core, origin, q), ring_send.at[q], ring_recv.at[r, q, s],
            device_id={"dp": (right, left)[r]}, device_id_type=MESH,
        ).start()

    def send_sib(q, origin):
        pltpu.make_async_remote_copy(
            ring(core, origin, q), ring(core, origin, q), sib_send.at[q], sib_recv.at[q],
            device_id={"dp": sib}, device_id_type=MESH,
        ).start()

    def wait_ring(r, q, s, origin):
        there = ring(core, origin, q)
        pltpu.make_async_copy(there, there, ring_recv.at[r, q, s - 1]).wait()

    def origin_of(r, s):
        return (p + chips - s) % chips if r == 0 else (p + s) % chips

    def first_hop(q):
        send_ring(0, q, 0, p)
        send_ring(1, q, 0, p)
        send_sib(q, p)

    slots = 2 * hops
    sends = CHUNKS * hops

    def comm(t):
        s = (t % slots) // 2
        q = 2 * (t // slots) + t % 2

        @pl.when(s == 0)
        def _():
            @pl.when(t < sends)
            def _():
                first_hop(q)

            @pl.when(t >= slots)
            def _():
                far = origin_of(0, hops)
                there = ring(core, far, q - 2)
                pltpu.make_async_copy(there, there, ring_recv.at[core, q - 2, hops - 1]).wait()
                send_sib(q - 2, far)

        @pl.when((s > 0) & (t < sends))
        def _():
            for r in range(2):
                origin = origin_of(r, s)
                wait_ring(r, q, s, origin)

                @pl.when(s < reach[r])
                def _():
                    send_ring(r, q, s, origin)

                send_sib(q, origin)

    first_hop(0)
    first_hop(1)

    @pl.loop(1, n)
    def _(i):
        pltpu.make_async_remote_copy(
            scales.at[me], scales.at[me], scale_send, scale_recv,
            device_id={"dp": (me + i) % n}, device_id_type=MESH,
        ).start()

    gate_acc[...] = jnp.zeros_like(gate_acc)
    up_acc[...] = jnp.zeros_like(up_acc)

    def compute(g):
        q = g // hops

        @pl.when(g == 0)
        def _():
            most = scales.at[pl.ds(0, n - 1)]
            pltpu.make_async_copy(most, most, scale_recv).wait()

        @pl.when(g % hops == 0)
        def _():
            for copy in weight_copies(q):
                copy.wait()
            there = raw.at[1 - core, :, :, pl.ds(q * depth, depth)]
            pltpu.make_async_copy(there, there, sib_recv.at[q]).wait()

        here = pl.ds(pl.multiple_of(g * part, 128), part)
        gains = gain[:, here]
        pieces = []
        for d in range(n):
            wide = raw[d % 2, place_of(d // 2, chips), :, here].astype(F32)
            scale = jnp.concatenate([scales[d]] * (part // 128), axis=1)
            pieces.append(wide * scale * gains)
        normed = jnp.concatenate(pieces, axis=0).astype(BF16)
        gate_acc[...] += jnp.dot(normed, gate_v[here, :], preferred_element_type=F32)
        up_acc[...] += jnp.dot(normed, up_v[here, :], preferred_element_type=F32)

    lag = slots + 1

    @pl.loop(2, sends + lag)
    def _(t):
        @pl.when(t == slots)
        def _():
            for q in range(EARLY, CHUNKS):
                for copy in weight_copies(q):
                    copy.start()

        @pl.when(t == 2 * slots)
        def _():
            for i in range(DOWN_LOADS // 2):
                down_copy(i).start()

        @pl.when(t == 3 * slots)
        def _():
            for i in range(DOWN_LOADS // 2, DOWN_LOADS):
                down_copy(i).start()

        @pl.when(t < sends + 2)
        def _():
            comm(t)

        @pl.when(t >= lag)
        def _():
            compute(t - lag)

    gates = gate_acc[...]
    hidden = (gates / (1.0 + jnp.exp(-gates)) * up_acc[...]).astype(BF16)
    for e in range(parts):
        hid[core, p, e] = hidden[:, e * ffe : (e + 1) * ffe]

    def send_hid(r, e, s, origin):
        there = hid.at[core, origin, e]
        pltpu.make_async_remote_copy(
            there, there, hid_send, hid_recv.at[r, e, s],
            device_id={"dp": (right, left)[r]}, device_id_type=MESH,
        ).start()

    def send_hidsib(e, s, origin):
        there = hid.at[core, origin, e]
        pltpu.make_async_remote_copy(
            there, there, hidsib_send, hidsib_recv.at[e, s],
            device_id={"dp": sib}, device_id_type=MESH,
        ).start()

    for e in range(parts):
        send_hid(0, e, 0, p)
        send_hid(1, e, 0, p)
        send_hidsib(e, 0, p)
    for i in range(DOWN_LOADS):
        down_copy(i).wait()
    acc[...] = jnp.zeros_like(acc)

    def add_block(origin, e):
        first = 2 * chip_at(origin, chips)
        for k in range(2):
            here = pl.ds(pl.multiple_of((first + k) * ffl + e * ffe, 128), ffe)
            acc[...] += jnp.dot(hid[k, origin, e], down_v[here, :], preferred_element_type=F32)

    def wait_hidsib(e, u, blocks):
        there = hid.at[0, pl.ds(0, blocks), e]
        pltpu.make_async_copy(there, there, hidsib_recv.at[e, u]).wait()

    @pl.loop(1, hops + 2)
    def _(s):
        u = s - 1
        for e in range(parts):
            @pl.when(s < hops)
            def _():
                for r in range(2):
                    origin = origin_of(r, s)
                    there = hid.at[core, origin, e]
                    pltpu.make_async_copy(there, there, hid_recv.at[r, e, s - 1]).wait()

                    @pl.when(s < reach[r])
                    def _():
                        send_hid(r, e, s, origin)

                    send_hidsib(e, s, origin)

            @pl.when(s == hops)
            def _():
                far = origin_of(0, hops)
                there = hid.at[core, far, e]
                pltpu.make_async_copy(there, there, hid_recv.at[core, e, hops - 1]).wait()
                send_hidsib(e, hops, far)

            @pl.when((u == 0) | (u == hops))
            def _():
                wait_hidsib(e, u, 1)

            @pl.when((u > 0) & (u < hops))
            def _():
                wait_hidsib(e, u, 2)
                add_block(origin_of(1, u), e)

            add_block(origin_of(0, u), e)

    mine = pl.ds(pl.multiple_of(me * cols, 128), cols)
    for d in range(n):
        wide = raw[d % 2, place_of(d // 2, chips), :, mine].astype(F32)
        stage[d] = (wide + acc[d * rows : (d + 1) * rows, :]).astype(BF16)

    @pl.loop(1, n)
    def _(i):
        peer = (me + i) % n
        pltpu.make_async_remote_copy(
            stage.at[peer], out.at[:, mine], out_send, out_recv,
            device_id={"dp": peer}, device_id_type=MESH,
        ).start()

    keep = pltpu.make_async_copy(stage.at[me], out.at[:, mine], out_own)
    keep.start()

    most = scales.at[pl.ds(0, n - 1)]
    pltpu.make_async_copy(most, most, scale_send).wait()
    for q in range(CHUNKS):
        there = raw.at[0, pl.ds(0, chips - 1), :, pl.ds(q * depth, depth)]
        pltpu.make_async_copy(there, there, ring_send.at[q]).wait()
        there = raw.at[0, :, :, pl.ds(q * depth, depth)]
        pltpu.make_async_copy(there, there, sib_send.at[q]).wait()
    there = hid.at[0, pl.ds(0, chips - 1)]
    pltpu.make_async_copy(there, there, hid_send).wait()
    there = hid.at[0]
    pltpu.make_async_copy(there, there, hidsib_send).wait()
    keep.wait()
    there = stage.at[pl.ds(0, n - 1)]
    pltpu.make_async_copy(there, there, out_send).wait()
    pltpu.make_async_copy(there, there, out_recv).wait()


def shards(n, tokens, gain, gate_weight, up_weight, down_weight):
    rows, width = tokens.shape
    ffl = gate_weight.shape[1]
    ff, cols = down_weight.shape
    chips = n // 2
    hops = chips // 2
    parts = 2 if ffl >= 256 else 1
    total_rows = n * rows
    dma = pltpu.SemaphoreType.DMA
    hbm = pl.BlockSpec(memory_space=pl.ANY)
    wide_gain = gain.astype(F32).reshape(1, width)
    return pl.pallas_call(
        functools.partial(block_kernel, n),
        out_shape=jax.ShapeDtypeStruct((rows, width), BF16),
        in_specs=[hbm, pl.BlockSpec(memory_space=pltpu.VMEM), hbm, hbm, hbm],
        out_specs=hbm,
        scratch_shapes=[
            pltpu.VMEM((2, chips, rows, width), BF16),
            pltpu.VMEM((n, rows, 128), F32),
            pltpu.VMEM((width, ffl), BF16),
            pltpu.VMEM((width, ffl), BF16),
            pltpu.VMEM((ff, cols), BF16),
            pltpu.VMEM((total_rows, ffl), F32),
            pltpu.VMEM((total_rows, ffl), F32),
            pltpu.VMEM((2, chips, parts, total_rows, ffl // parts), BF16),
            pltpu.VMEM((total_rows, cols), F32),
            pltpu.VMEM((n, rows, cols), BF16),
            dma(()),
            dma((CHUNKS,)),
            dma((CHUNKS,)),
            dma((DOWN_LOADS,)),
            dma(()),
            dma(()),
            dma((2, CHUNKS, hops)),
            dma((CHUNKS,)),
            dma((CHUNKS,)),
            dma((CHUNKS,)),
            dma((2, parts, hops)),
            dma(()),
            dma((parts, hops + 1)),
            dma(()),
            dma(()),
            dma(()),
            dma(()),
        ],
        compiler_params=pltpu.CompilerParams(
            collective_id=0, has_side_effects=True, vmem_limit_bytes=62 * 1024 * 1024
        ),
        cost_estimate=pl.CostEstimate(
            flops=2 * total_rows * (2 * width * ffl + ff * cols),
            bytes_accessed=2 * (2 * width * ffl + ff * cols),
            transcendentals=total_rows * ffl,
        ),
        name="swiglu_block",
    )(tokens, wide_gain, gate_weight, up_weight, down_weight)


def solution(mesh):
    return jax.shard_map(
        functools.partial(shards, mesh.shape["dp"]),
        mesh=mesh,
        in_specs=(P(("groups", "dp"), None), P(), P(None, "dp"), P(None, "dp"), P(None, "dp")),
        out_specs=P(("groups", "dp"), None),
        check_vma=False,
    )
```

```python
import functools

import jax
import jax.numpy as jnp
from jax import lax
from jax.experimental import pallas as pl
from jax.experimental.pallas import tpu as pltpu
from jax.sharding import PartitionSpec as P

MESH = pl.DeviceIdType.MESH
CHUNKS = 4
EARLY = 2
DOWN_LOADS = 4
LEAD = 2
STAGGER = 1
F32 = jnp.float32
BF16 = jnp.bfloat16


def chip_at(place, chips):
    if chips > 8:
        return place
    half = chips // 2
    back = place // half
    return (1 - back) * 2 * place + back * (2 * (chips - 1 - place) + 1)


def place_of(chip, chips):
    if chips > 8:
        return chip
    odd, rank = chip % 2, chip // 2
    return rank + odd * (chips - 1 - 2 * rank)


def block_kernel(
    n,
    tokens, gain, gate, up, down, out,
    raw, scales, gate_v, up_v, down_v, gate_acc, up_acc, hid, acc, stage,
    own_sem, gate_sem, up_sem, down_sem, scale_send, scale_recv,
    ring_recv, ring_send, sib_recv, sib_send,
    hid_recv, hid_send, hidsib_recv, hidsib_send,
    out_send, out_recv, out_own,
):
    chips = n // 2
    hops = chips // 2
    rows, width = tokens.shape
    ffl = gate.shape[1]
    cols = down.shape[1]
    depth = width // CHUNKS
    part = depth // hops
    total_rows = n * rows
    parts = hid.shape[2]
    ffe = ffl // parts
    down_rows = down.shape[0] // DOWN_LOADS

    me = lax.axis_index("dp")
    core = me % 2
    p = place_of(me // 2, chips)
    sib = me + 1 - 2 * core
    right = 2 * chip_at((p + 1) % chips, chips) + core
    left = 2 * chip_at((p + chips - 1) % chips, chips) + core
    reach = (hops - core, hops - 1 + core)

    own = pltpu.make_async_copy(tokens, raw.at[core, p], own_sem)
    own.start()

    def weight_copies(q):
        here = pl.ds(q * depth, depth)
        return (
            pltpu.make_async_copy(gate.at[here], gate_v.at[here], gate_sem.at[q]),
            pltpu.make_async_copy(up.at[here], up_v.at[here], up_sem.at[q]),
        )

    def down_copy(i):
        here = pl.ds(i * down_rows, down_rows)
        return pltpu.make_async_copy(down.at[here], down_v.at[here], down_sem.at[i])

    barrier = pltpu.get_barrier_semaphore()

    @pl.loop(1, n)
    def _(i):
        pl.semaphore_signal(barrier, inc=1, device_id={"dp": (me + i) % n}, device_id_type=MESH)

    for q in range(EARLY):
        for copy in weight_copies(q):
            copy.start()

    own.wait()
    squares = jnp.zeros((rows, 128), F32)
    step = 2048

    def add_squares(i, squares):
        wide = raw[core, p, :, pl.ds(i * step, step)].astype(F32)
        wide = wide * wide
        for b in range(step // 128):
            squares = squares + wide[:, b * 128 : (b + 1) * 128]
        return squares

    squares = lax.fori_loop(0, width // step, add_squares, squares)
    mean = jnp.sum(squares, axis=1, keepdims=True) / width
    scales[me] = jnp.broadcast_to(lax.rsqrt(mean + 1e-05), (rows, 128))
    pl.semaphore_wait(barrier, n - 1)

    def ring(k, origin, q):
        return raw.at[k, origin, :, pl.ds(q * depth, depth)]

    def send_ring(r, q, s, origin):
        pltpu.make_async_remote_copy(
            ring(core, origin, q), ring(core, origin, q), ring_send.at[q], ring_recv.at[r, q, s],
            device_id={"dp": (right, left)[r]}, device_id_type=MESH,
        ).start()

    def send_sib(q, origin):
        pltpu.make_async_remote_copy(
            ring(core, origin, q), ring(core, origin, q), sib_send.at[q], sib_recv.at[q],
            device_id={"dp": sib}, device_id_type=MESH,
        ).start()

    def wait_ring(r, q, s, origin):
        there = ring(core, origin, q)
        pltpu.make_async_copy(there, there, ring_recv.at[r, q, s - 1]).wait()

    def origin_of(r, s):
        return (p + chips - s) % chips if r == 0 else (p + s) % chips

    def first_hop(q):
        send_ring(0, q, 0, p)
        send_ring(1, q, 0, p)
        send_sib(q, p)

    def comm(q, s):
        @pl.when(s < hops)
        def _():
            for r in range(2):
                origin = origin_of(r, s)
                wait_ring(r, q, s, origin)

                @pl.when(s < reach[r])
                def _():
                    send_ring(r, q, s, origin)

                send_sib(q, origin)

        @pl.when(s == hops)
        def _():
            far = origin_of(0, hops)
            wait_ring(core, q, hops, far)
            send_sib(q, far)

    for q in range(LEAD + 1):
        first_hop(q)

    @pl.loop(1, n)
    def _(i):
        pltpu.make_async_remote_copy(
            scales.at[me], scales.at[me], scale_send, scale_recv,
            device_id={"dp": (me + i) % n}, device_id_type=MESH,
        ).start()

    gate_acc[...] = jnp.zeros_like(gate_acc)
    up_acc[...] = jnp.zeros_like(up_acc)

    def compute(g):
        q = g // hops

        @pl.when(g == 0)
        def _():
            most = scales.at[pl.ds(0, n - 1)]
            pltpu.make_async_copy(most, most, scale_recv).wait()

        @pl.when(g % hops == 0)
        def _():
            for copy in weight_copies(q):
                copy.wait()
            there = raw.at[1 - core, :, :, pl.ds(q * depth, depth)]
            pltpu.make_async_copy(there, there, sib_recv.at[q]).wait()

        here = pl.ds(pl.multiple_of(g * part, 128), part)
        gains = gain[:, here]
        pieces = []
        for d in range(n):
            wide = raw[d % 2, place_of(d // 2, chips), :, here].astype(F32)
            scale = jnp.concatenate([scales[d]] * (part // 128), axis=1)
            pieces.append(wide * scale * gains)
        normed = jnp.concatenate(pieces, axis=0).astype(BF16)
        gate_acc[...] += jnp.dot(normed, gate_v[here, :], preferred_element_type=F32)
        up_acc[...] += jnp.dot(normed, up_v[here, :], preferred_element_type=F32)

    @pl.loop(1, CHUNKS + STAGGER * hops + 1)
    def _(t):
        @pl.when(t + LEAD < CHUNKS)
        def _():
            first_hop(t + LEAD)

        @pl.when(t <= CHUNKS - EARLY)
        def _():
            for copy in weight_copies(t + EARLY - 1):
                copy.start()

        @pl.when((t > CHUNKS - EARLY) & (t <= CHUNKS - EARLY + DOWN_LOADS))
        def _():
            down_copy(t - (CHUNKS - EARLY) - 1).start()

        @pl.loop(1, hops + 1)
        def _(s):
            q = t - STAGGER * s

            @pl.when((q >= 0) & (q < CHUNKS))
            def _():
                comm(q, s)

            @pl.when(t > STAGGER * hops)
            def _():
                compute((t - STAGGER * hops - 1) * hops + s - 1)

    gates = gate_acc[...]
    hidden = (gates / (1.0 + jnp.exp(-gates)) * up_acc[...]).astype(BF16)
    for e in range(parts):
        hid[core, p, e] = hidden[:, e * ffe : (e + 1) * ffe]

    def send_hid(r, e, s, origin):
        there = hid.at[core, origin, e]
        pltpu.make_async_remote_copy(
            there, there, hid_send, hid_recv.at[r, e, s],
            device_id={"dp": (right, left)[r]}, device_id_type=MESH,
        ).start()

    def send_hidsib(e, s, origin):
        there = hid.at[core, origin, e]
        pltpu.make_async_remote_copy(
            there, there, hidsib_send, hidsib_recv.at[e, s],
            device_id={"dp": sib}, device_id_type=MESH,
        ).start()

    for e in range(parts):
        send_hid(0, e, 0, p)
        send_hid(1, e, 0, p)
        send_hidsib(e, 0, p)
    for i in range(DOWN_LOADS):
        down_copy(i).wait()
    acc[...] = jnp.zeros_like(acc)

    group = 2 if parts > 1 else 1

    def add_block(origin, e):
        first = 2 * chip_at(origin, chips)
        total = acc[...]
        for k in range(2):
            here = pl.ds(pl.multiple_of((first + k) * ffl + e * ffe, 128), group * ffe)
            block = jnp.concatenate([hid[k, origin, e + i] for i in range(group)], axis=1)
            total += jnp.dot(block, down_v[here, :], preferred_element_type=F32)
        acc[...] = total

    def wait_hidsib(e, u, blocks):
        there = hid.at[0, pl.ds(0, blocks), e]
        pltpu.make_async_copy(there, there, hidsib_recv.at[e, u]).wait()

    @pl.loop(1, hops + 2)
    def _(s):
        u = s - 1

        def hop(e):
            @pl.when(s < hops)
            def _():
                for r in range(2):
                    origin = origin_of(r, s)
                    there = hid.at[core, origin, e]
                    pltpu.make_async_copy(there, there, hid_recv.at[r, e, s - 1]).wait()

                    @pl.when(s < reach[r])
                    def _():
                        send_hid(r, e, s, origin)

                    send_hidsib(e, s, origin)

            @pl.when(s == hops)
            def _():
                far = origin_of(0, hops)
                there = hid.at[core, far, e]
                pltpu.make_async_copy(there, there, hid_recv.at[core, e, hops - 1]).wait()
                send_hidsib(e, hops, far)

            @pl.when((u == 0) | (u == hops))
            def _():
                wait_hidsib(e, u, 1)

            @pl.when((u > 0) & (u < hops))
            def _():
                wait_hidsib(e, u, 2)

        for e in range(0, parts, group):
            for i in range(group):
                hop(e + i)

            @pl.when((u > 0) & (u < hops))
            def _():
                add_block(origin_of(1, u), e)

            add_block(origin_of(0, u), e)

    mine = pl.ds(pl.multiple_of(me * cols, 128), cols)
    for d in range(n):
        wide = raw[d % 2, place_of(d // 2, chips), :, mine].astype(F32)
        stage[d] = (wide + acc[d * rows : (d + 1) * rows, :]).astype(BF16)

    @pl.loop(1, n)
    def _(i):
        peer = (me + i) % n
        pltpu.make_async_remote_copy(
            stage.at[peer], out.at[:, mine], out_send, out_recv,
            device_id={"dp": peer}, device_id_type=MESH,
        ).start()

    keep = pltpu.make_async_copy(stage.at[me], out.at[:, mine], out_own)
    keep.start()

    most = scales.at[pl.ds(0, n - 1)]
    pltpu.make_async_copy(most, most, scale_send).wait()
    for q in range(CHUNKS):
        there = raw.at[0, pl.ds(0, chips - 1), :, pl.ds(q * depth, depth)]
        pltpu.make_async_copy(there, there, ring_send.at[q]).wait()
        there = raw.at[0, :, :, pl.ds(q * depth, depth)]
        pltpu.make_async_copy(there, there, sib_send.at[q]).wait()
    there = hid.at[0, pl.ds(0, chips - 1)]
    pltpu.make_async_copy(there, there, hid_send).wait()
    there = hid.at[0]
    pltpu.make_async_copy(there, there, hidsib_send).wait()
    keep.wait()
    there = stage.at[pl.ds(0, n - 1)]
    pltpu.make_async_copy(there, there, out_send).wait()
    pltpu.make_async_copy(there, there, out_recv).wait()


def shards(n, tokens, gain, gate_weight, up_weight, down_weight):
    rows, width = tokens.shape
    ffl = gate_weight.shape[1]
    ff, cols = down_weight.shape
    chips = n // 2
    hops = chips // 2
    parts = 4 if ffl % 512 == 0 else 1
    total_rows = n * rows
    dma = pltpu.SemaphoreType.DMA
    hbm = pl.BlockSpec(memory_space=pl.ANY)
    wide_gain = gain.astype(F32).reshape(1, width)
    return pl.pallas_call(
        functools.partial(block_kernel, n),
        out_shape=jax.ShapeDtypeStruct((rows, width), BF16),
        in_specs=[hbm, pl.BlockSpec(memory_space=pltpu.VMEM), hbm, hbm, hbm],
        out_specs=hbm,
        scratch_shapes=[
            pltpu.VMEM((2, chips, rows, width), BF16),
            pltpu.VMEM((n, rows, 128), F32),
            pltpu.VMEM((width, ffl), BF16),
            pltpu.VMEM((width, ffl), BF16),
            pltpu.VMEM((ff, cols), BF16),
            pltpu.VMEM((total_rows, ffl), F32),
            pltpu.VMEM((total_rows, ffl), F32),
            pltpu.VMEM((2, chips, parts, total_rows, ffl // parts), BF16),
            pltpu.VMEM((total_rows, cols), F32),
            pltpu.VMEM((n, rows, cols), BF16),
            dma(()),
            dma((CHUNKS,)),
            dma((CHUNKS,)),
            dma((DOWN_LOADS,)),
            dma(()),
            dma(()),
            dma((2, CHUNKS, hops)),
            dma((CHUNKS,)),
            dma((CHUNKS,)),
            dma((CHUNKS,)),
            dma((2, parts, hops)),
            dma(()),
            dma((parts, hops + 1)),
            dma(()),
            dma(()),
            dma(()),
            dma(()),
        ],
        compiler_params=pltpu.CompilerParams(
            collective_id=0, has_side_effects=True, vmem_limit_bytes=62 * 1024 * 1024
        ),
        cost_estimate=pl.CostEstimate(
            flops=2 * total_rows * (2 * width * ffl + ff * cols),
            bytes_accessed=2 * (2 * width * ffl + ff * cols),
            transcendentals=total_rows * ffl,
        ),
        name="swiglu_block",
    )(tokens, wide_gain, gate_weight, up_weight, down_weight)


def solution(mesh):
    return jax.shard_map(
        functools.partial(shards, mesh.shape["dp"]),
        mesh=mesh,
        in_specs=(P(("groups", "dp"), None), P(), P(None, "dp"), P(None, "dp"), P(None, "dp")),
        out_specs=P(("groups", "dp"), None),
        check_vma=False,
    )
```

```python
import functools

import jax
import jax.numpy as jnp
from jax import lax
from jax.experimental import pallas as pl
from jax.experimental.pallas import tpu as pltpu
from jax.sharding import PartitionSpec as P

MESH = pl.DeviceIdType.MESH
CHUNKS = 4
EARLY = 2
DOWN_LOADS = 4
LEAD = 2
STAGGER = 1
F32 = jnp.float32
BF16 = jnp.bfloat16


def chip_at(place, chips):
    if chips > 8:
        return place
    half = chips // 2
    back = place // half
    return (1 - back) * 2 * place + back * (2 * (chips - 1 - place) + 1)


def place_of(chip, chips):
    if chips > 8:
        return chip
    odd, rank = chip % 2, chip // 2
    return rank + odd * (chips - 1 - 2 * rank)


def block_kernel(
    n,
    tokens, gain_in, gate, up, down, out, gain,
    raw, scales, gate_v, up_v, down_v, gate_acc, up_acc, hid, acc, stage,
    own_sem, gate_sem, up_sem, down_sem, scale_send, scale_recv,
    ring_recv, ring_send, sib_recv, sib_send,
    hid_recv, hid_send, hidsib_recv, hidsib_send,
    out_send, out_recv, out_own,
):
    chips = n // 2
    hops = chips // 2
    rows, width = tokens.shape
    ffl = gate.shape[1]
    cols = down.shape[1]
    depth = width // CHUNKS
    part = depth // hops
    total_rows = n * rows
    parts = hid.shape[2]
    ffe = ffl // parts
    down_rows = down.shape[0] // DOWN_LOADS

    me = lax.axis_index("dp")
    core = me % 2
    p = place_of(me // 2, chips)
    sib = me + 1 - 2 * core
    right = 2 * chip_at((p + 1) % chips, chips) + core
    left = 2 * chip_at((p + chips - 1) % chips, chips) + core
    reach = (hops - core, hops - 1 + core)

    own = pltpu.make_async_copy(tokens, raw.at[core, p], own_sem)
    own.start()

    def weight_copies(q):
        here = pl.ds(q * depth, depth)
        return (
            pltpu.make_async_copy(gate.at[here], gate_v.at[here], gate_sem.at[q]),
            pltpu.make_async_copy(up.at[here], up_v.at[here], up_sem.at[q]),
        )

    def down_copy(i):
        here = pl.ds(i * down_rows, down_rows)
        return pltpu.make_async_copy(down.at[here], down_v.at[here], down_sem.at[i])

    barrier = pltpu.get_barrier_semaphore()

    @pl.loop(1, n)
    def _(i):
        pl.semaphore_signal(barrier, inc=1, device_id={"dp": (me + i) % n}, device_id_type=MESH)

    for q in range(EARLY):
        for copy in weight_copies(q):
            copy.start()

    gain[...] = gain_in[...].astype(F32).reshape(1, width)
    own.wait()
    squares = jnp.zeros((rows, 128), F32)
    step = 2048

    def add_squares(i, squares):
        wide = raw[core, p, :, pl.ds(i * step, step)].astype(F32)
        wide = wide * wide
        for b in range(step // 128):
            squares = squares + wide[:, b * 128 : (b + 1) * 128]
        return squares

    squares = lax.fori_loop(0, width // step, add_squares, squares)
    mean = jnp.sum(squares, axis=1, keepdims=True) / width
    scales[me] = jnp.broadcast_to(lax.rsqrt(mean + 1e-05), (rows, 128))
    pl.semaphore_wait(barrier, n - 1)

    def ring(k, origin, q):
        return raw.at[k, origin, :, pl.ds(q * depth, depth)]

    def send_ring(r, q, s, origin):
        pltpu.make_async_remote_copy(
            ring(core, origin, q), ring(core, origin, q), ring_send.at[q], ring_recv.at[r, q, s],
            device_id={"dp": (right, left)[r]}, device_id_type=MESH,
        ).start()

    def send_sib(q, origin):
        pltpu.make_async_remote_copy(
            ring(core, origin, q), ring(core, origin, q), sib_send.at[q], sib_recv.at[q],
            device_id={"dp": sib}, device_id_type=MESH,
        ).start()

    def wait_ring(r, q, s, origin):
        there = ring(core, origin, q)
        pltpu.make_async_copy(there, there, ring_recv.at[r, q, s - 1]).wait()

    def origin_of(r, s):
        return (p + chips - s) % chips if r == 0 else (p + s) % chips

    def first_hop(q):
        send_ring(0, q, 0, p)
        send_ring(1, q, 0, p)
        send_sib(q, p)

    def comm(q, s):
        @pl.when(s < hops)
        def _():
            for r in range(2):
                origin = origin_of(r, s)
                wait_ring(r, q, s, origin)

                @pl.when(s < reach[r])
                def _():
                    send_ring(r, q, s, origin)

                send_sib(q, origin)

        @pl.when(s == hops)
        def _():
            far = origin_of(0, hops)
            wait_ring(core, q, hops, far)
            send_sib(q, far)

    for q in range(LEAD + 1):
        first_hop(q)

    @pl.loop(1, n)
    def _(i):
        pltpu.make_async_remote_copy(
            scales.at[me], scales.at[me], scale_send, scale_recv,
            device_id={"dp": (me + i) % n}, device_id_type=MESH,
        ).start()

    gate_acc[...] = jnp.zeros_like(gate_acc)
    up_acc[...] = jnp.zeros_like(up_acc)

    def compute(g):
        q = g // hops

        @pl.when(g == 0)
        def _():
            most = scales.at[pl.ds(0, n - 1)]
            pltpu.make_async_copy(most, most, scale_recv).wait()

        @pl.when(g % hops == 0)
        def _():
            for copy in weight_copies(q):
                copy.wait()
            there = raw.at[1 - core, :, :, pl.ds(q * depth, depth)]
            pltpu.make_async_copy(there, there, sib_recv.at[q]).wait()

        here = pl.ds(pl.multiple_of(g * part, 128), part)
        gains = gain[:, here]
        pieces = []
        for d in range(n):
            wide = raw[d % 2, place_of(d // 2, chips), :, here].astype(F32)
            scale = jnp.concatenate([scales[d]] * (part // 128), axis=1)
            pieces.append(wide * scale * gains)
        normed = jnp.concatenate(pieces, axis=0).astype(BF16)
        gate_acc[...] += jnp.dot(normed, gate_v[here, :], preferred_element_type=F32)
        up_acc[...] += jnp.dot(normed, up_v[here, :], preferred_element_type=F32)

    @pl.loop(1, CHUNKS + STAGGER * hops + 1)
    def _(t):
        @pl.when(t + LEAD < CHUNKS)
        def _():
            first_hop(t + LEAD)

        @pl.when(t <= CHUNKS - EARLY)
        def _():
            for copy in weight_copies(t + EARLY - 1):
                copy.start()

        @pl.when((t > CHUNKS - EARLY) & (t <= CHUNKS - EARLY + DOWN_LOADS))
        def _():
            down_copy(t - (CHUNKS - EARLY) - 1).start()

        @pl.loop(1, hops + 1)
        def _(s):
            q = t - STAGGER * s

            @pl.when((q >= 0) & (q < CHUNKS))
            def _():
                comm(q, s)

            @pl.when(t > STAGGER * hops)
            def _():
                compute((t - STAGGER * hops - 1) * hops + s - 1)

    gates = gate_acc[...]
    hidden = (gates / (1.0 + jnp.exp(-gates)) * up_acc[...]).astype(BF16)
    for e in range(parts):
        hid[core, p, e] = hidden[:, e * ffe : (e + 1) * ffe]

    def send_hid(r, e, s, origin):
        there = hid.at[core, origin, e]
        pltpu.make_async_remote_copy(
            there, there, hid_send, hid_recv.at[r, e, s],
            device_id={"dp": (right, left)[r]}, device_id_type=MESH,
        ).start()

    def send_hidsib(e, s, origin):
        there = hid.at[core, origin, e]
        pltpu.make_async_remote_copy(
            there, there, hidsib_send, hidsib_recv.at[e, s],
            device_id={"dp": sib}, device_id_type=MESH,
        ).start()

    for e in range(parts):
        send_hid(0, e, 0, p)
        send_hid(1, e, 0, p)
        send_hidsib(e, 0, p)
    for i in range(DOWN_LOADS):
        down_copy(i).wait()
    acc[...] = jnp.zeros_like(acc)

    group = 2 if parts > 1 else 1

    def add_block(origin, e):
        first = 2 * chip_at(origin, chips)
        total = acc[...]
        for k in range(2):
            here = pl.ds(pl.multiple_of((first + k) * ffl + e * ffe, 128), group * ffe)
            block = jnp.concatenate([hid[k, origin, e + i] for i in range(group)], axis=1)
            total += jnp.dot(block, down_v[here, :], preferred_element_type=F32)
        acc[...] = total

    def wait_hidsib(e, u, blocks):
        there = hid.at[0, pl.ds(0, blocks), e]
        pltpu.make_async_copy(there, there, hidsib_recv.at[e, u]).wait()

    @pl.loop(1, hops + 2)
    def _(s):
        u = s - 1

        def hop(e):
            @pl.when(s < hops)
            def _():
                for r in range(2):
                    origin = origin_of(r, s)
                    there = hid.at[core, origin, e]
                    pltpu.make_async_copy(there, there, hid_recv.at[r, e, s - 1]).wait()

                    @pl.when(s < reach[r])
                    def _():
                        send_hid(r, e, s, origin)

                    send_hidsib(e, s, origin)

            @pl.when(s == hops)
            def _():
                far = origin_of(0, hops)
                there = hid.at[core, far, e]
                pltpu.make_async_copy(there, there, hid_recv.at[core, e, hops - 1]).wait()
                send_hidsib(e, hops, far)

            @pl.when((u == 0) | (u == hops))
            def _():
                wait_hidsib(e, u, 1)

            @pl.when((u > 0) & (u < hops))
            def _():
                wait_hidsib(e, u, 2)

        for e in range(0, parts, group):
            for i in range(group):
                hop(e + i)

            @pl.when((u > 0) & (u < hops))
            def _():
                add_block(origin_of(1, u), e)

            add_block(origin_of(0, u), e)

    mine = pl.ds(pl.multiple_of(me * cols, 128), cols)
    for d in range(n):
        wide = raw[d % 2, place_of(d // 2, chips), :, mine].astype(F32)
        stage[d] = (wide + acc[d * rows : (d + 1) * rows, :]).astype(BF16)

    @pl.loop(1, n)
    def _(i):
        peer = (me + i) % n
        pltpu.make_async_remote_copy(
            stage.at[peer], out.at[:, mine], out_send, out_recv,
            device_id={"dp": peer}, device_id_type=MESH,
        ).start()

    keep = pltpu.make_async_copy(stage.at[me], out.at[:, mine], out_own)
    keep.start()

    most = scales.at[pl.ds(0, n - 1)]
    pltpu.make_async_copy(most, most, scale_send).wait()
    for q in range(CHUNKS):
        there = raw.at[0, pl.ds(0, chips - 1), :, pl.ds(q * depth, depth)]
        pltpu.make_async_copy(there, there, ring_send.at[q]).wait()
        there = raw.at[0, :, :, pl.ds(q * depth, depth)]
        pltpu.make_async_copy(there, there, sib_send.at[q]).wait()
    there = hid.at[0, pl.ds(0, chips - 1)]
    pltpu.make_async_copy(there, there, hid_send).wait()
    there = hid.at[0]
    pltpu.make_async_copy(there, there, hidsib_send).wait()
    keep.wait()
    there = stage.at[pl.ds(0, n - 1)]
    pltpu.make_async_copy(there, there, out_send).wait()
    pltpu.make_async_copy(there, there, out_recv).wait()


def shards(n, tokens, gain, gate_weight, up_weight, down_weight):
    rows, width = tokens.shape
    ffl = gate_weight.shape[1]
    ff, cols = down_weight.shape
    chips = n // 2
    hops = chips // 2
    parts = 4 if ffl % 512 == 0 else 1
    total_rows = n * rows
    dma = pltpu.SemaphoreType.DMA
    hbm = pl.BlockSpec(memory_space=pl.ANY)
    return pl.pallas_call(
        functools.partial(block_kernel, n),
        out_shape=jax.ShapeDtypeStruct((rows, width), BF16),
        in_specs=[hbm, pl.BlockSpec(memory_space=pltpu.VMEM), hbm, hbm, hbm],
        out_specs=hbm,
        scratch_shapes=[
            pltpu.VMEM((1, width), F32),
            pltpu.VMEM((2, chips, rows, width), BF16),
            pltpu.VMEM((n, rows, 128), F32),
            pltpu.VMEM((width, ffl), BF16),
            pltpu.VMEM((width, ffl), BF16),
            pltpu.VMEM((ff, cols), BF16),
            pltpu.VMEM((total_rows, ffl), F32),
            pltpu.VMEM((total_rows, ffl), F32),
            pltpu.VMEM((2, chips, parts, total_rows, ffl // parts), BF16),
            pltpu.VMEM((total_rows, cols), F32),
            pltpu.VMEM((n, rows, cols), BF16),
            dma(()),
            dma((CHUNKS,)),
            dma((CHUNKS,)),
            dma((DOWN_LOADS,)),
            dma(()),
            dma(()),
            dma((2, CHUNKS, hops)),
            dma((CHUNKS,)),
            dma((CHUNKS,)),
            dma((CHUNKS,)),
            dma((2, parts, hops)),
            dma(()),
            dma((parts, hops + 1)),
            dma(()),
            dma(()),
            dma(()),
            dma(()),
        ],
        compiler_params=pltpu.CompilerParams(
            collective_id=0, has_side_effects=True, vmem_limit_bytes=62 * 1024 * 1024
        ),
        cost_estimate=pl.CostEstimate(
            flops=2 * total_rows * (2 * width * ffl + ff * cols),
            bytes_accessed=2 * (2 * width * ffl + ff * cols),
            transcendentals=total_rows * ffl,
        ),
        name="swiglu_block",
    )(tokens, gain, gate_weight, up_weight, down_weight)


def solution(mesh):
    return jax.shard_map(
        functools.partial(shards, mesh.shape["dp"]),
        mesh=mesh,
        in_specs=(P(("groups", "dp"), None), P(), P(None, "dp"), P(None, "dp"), P(None, "dp")),
        out_specs=P(("groups", "dp"), None),
        check_vma=False,
    )
```
